32 devices in a mesh: blk: 8 (over z, x), xor: 4 (over y, core).
Axes of the slice: x: 2, y: 2, z: 4, core: 2. Of those that a mesh axis runs over, the one named last changes fastest.
Arguments:
- users: float32 [32768, 256], P(('blk', 'xor')), may hold values from -1.5 to 1.5
- user_accum: float32 [32768, 256], P(('blk', 'xor')), may hold values from 0.05 to 1
- items: float32 [16384, 256], P(('blk', 'xor')), may hold values from -1.5 to 1.5
- item_accum: float32 [16384, 256], P(('blk', 'xor')), may hold values from 0.05 to 1
- seen_user: int32 [6, 512], P(None, ('blk', 'xor')), may hold values from 0 to 7
- seen_item: int32 [6, 512], P(None, ('blk', 'xor')), may hold values from 0 to 3
- row_live: int32 [6, 512, 128], P(None, ('blk', 'xor')), may hold values 0 or 1
- col_live: int32 [6, 512, 128], P(None, ('blk', 'xor')), may hold values 0 or 1
- neg_user: int32 [6, 256], P(None, ('blk', 'xor')), may hold values from 0 to 7
- neg_item: int32 [6, 256], P(None, ('blk', 'xor')), may hold values from 0 to 3
Outputs:
- users_out: float32 [32768, 256], P(('blk', 'xor'))
- user_accum_out: float32 [32768, 256], P(('blk', 'xor'))
- items_out: float32 [16384, 256], P(('blk', 'xor'))
- item_accum_out: float32 [16384, 256], P(('blk', 'xor'))
The draws below stay inside these ranges and needn't reach their ends.
All inputs are finite; a program needn't handle non-finite values. No bound on the sum of `row_live` or of `col_live` on one device may be relied on, other than what follows from the above.
Results may differ from the reference program's by a relative error of at most 0.0051.
Values sent between devices are 32-bit elements; how exact they have to be, the bound alone decides.
A program may use at most 64 MiB of HBM per device.

```python
import math
import jax
import jax.numpy as jnp
import numpy as np
from jax import lax

K = 256
TILE = 128
SUBS = 6
USER_DEV = 1024
ITEM_DEV = 512
OBS = 16
NEG = 8
HALF = 256
UT = 8
IT = 4
USERS = 32768
ITEMS = 16384
OBS_ALL = 512
NEG_ALL = 256
N_BLK = 8
N_XOR = 4


def touch_ends(entries, key, low, largest):
    longest = entries.shape.index(max(entries.shape))
    spots = []
    for shift in (0, 1):
        where = [jax.random.randint(jax.random.fold_in(key, axis), (), 0, length) for axis, length in enumerate(entries.shape)]
        where[longest] = (where[longest] + shift) % entries.shape[longest]
        spots.append(tuple(where))
    return entries.at[spots[0]].set(low).at[spots[1]].set(largest)


def levels(key, shape, split, low, high):
    def one(position, shards_of):
        steps = jax.random.uniform(jax.random.fold_in(jax.random.fold_in(key, 6), position), (shards_of,), jnp.float32, low / len(split), high / len(split))
        return jnp.repeat(jnp.exp(steps), shape[position] // shards_of).reshape((-1,) + (1,) * (len(shape) - position - 1))

    level = one(*split[0])
    for cut in split[1:]:
        level = level * one(*cut)
    return level


def bell_draw(rng, extent, deviation, most, shards=(), kind=jnp.bfloat16):
    drawn = jax.random.normal(rng, extent, jnp.float32) * deviation
    if len(shards) > 0:
        drawn = levels(rng, extent, shards, -0.22, 0.18) * drawn
    return jnp.clip(drawn, min=-most, max=most).astype(kind)


def setup_inputs(seed: int = 0) -> dict:
    streams_of = jax.random.split(jax.random.key(seed), 11)
    users = bell_draw(streams_of[0], (USERS, K), 0.25, 1.5, ((0, 32),), jnp.float32)
    user_accum = jnp.clip(jnp.exp(math.log(1.0) - 2.9957323 * jax.random.uniform(streams_of[1], (USERS, K), jnp.float32) ** levels(streams_of[1], (USERS, K), ((0, 32),), -0.2, 0.2)), 0.05, 1.0)
    items = bell_draw(streams_of[2], (ITEMS, K), 0.25, 1.5, ((0, 32),), jnp.float32)
    item_accum = jnp.clip(jnp.exp(math.log(1.0) - 2.9957323 * jax.random.uniform(streams_of[3], (ITEMS, K), jnp.float32) ** levels(streams_of[3], (ITEMS, K), ((0, 32),), -0.2, 0.2)), 0.05, 1.0)
    seen_user = touch_ends(jax.random.randint(streams_of[4], (SUBS, OBS_ALL), 0, UT), jax.random.fold_in(streams_of[4], 1), 0, UT - 1).astype(jnp.int32)
    seen_item = touch_ends(jax.random.randint(streams_of[5], (SUBS, OBS_ALL), 0, IT), jax.random.fold_in(streams_of[5], 1), 0, IT - 1).astype(jnp.int32)
    row_live = touch_ends((jax.random.randint(streams_of[6], (SUBS, OBS_ALL, TILE), 0, 4) < 3).astype(jnp.int32), jax.random.fold_in(streams_of[6], 1), 0, 1)
    col_live = touch_ends((jax.random.randint(streams_of[7], (SUBS, OBS_ALL, TILE), 0, 2) < 1).astype(jnp.int32), jax.random.fold_in(streams_of[7], 1), 0, 1)
    neg_user = touch_ends(jax.random.randint(streams_of[8], (SUBS, NEG_ALL), 0, UT), jax.random.fold_in(streams_of[8], 1), 0, UT - 1).astype(jnp.int32)
    neg_item = touch_ends(jax.random.randint(streams_of[9], (SUBS, NEG_ALL), 0, IT), jax.random.fold_in(streams_of[9], 1), 0, IT - 1).astype(jnp.int32)
    return dict(users=users, user_accum=user_accum, items=items, item_accum=item_accum, seen_user=seen_user, seen_item=seen_item, row_live=row_live, col_live=col_live, neg_user=neg_user, neg_item=neg_item)


LEARN_RATE = 0.05
DECAY = 0.02
NEG_WEIGHT = 0.25

def local_step(users, user_accum, items, item_accum, seen_user, seen_item, row_live, col_live, neg_user, neg_item):
    width = users.shape[1]
    user_bf = users.astype(jnp.bfloat16).reshape(-1, 128, width)
    item_bf = items.astype(jnp.bfloat16).reshape(-1, 128, width)
    tile_user = jnp.concatenate([seen_user, neg_user]).astype(jnp.int32)
    tile_item = jnp.concatenate([seen_item, neg_item]).astype(jnp.int32)
    user_tiles = user_bf[tile_user].astype(jnp.float32)
    item_tiles = item_bf[tile_item].astype(jnp.float32)
    observed = row_live.astype(jnp.float32)[:, :, None] * col_live.astype(jnp.float32)[:, None, :]
    negative = jnp.full((neg_user.shape[0], 128, 128), NEG_WEIGHT, jnp.float32)
    weight = jnp.concatenate([observed, negative])
    target = jnp.concatenate([jnp.ones((seen_user.shape[0], 1, 1), jnp.float32), jnp.zeros((neg_user.shape[0], 1, 1), jnp.float32)])
    scores = jnp.einsum('tik,tjk->tij', user_tiles, item_tiles)
    residual = (weight * (scores - target)).astype(jnp.bfloat16).astype(jnp.float32)
    user_terms = jnp.einsum('tij,tjk->tik', residual, item_tiles)
    item_terms = jnp.einsum('tij,tik->tjk', residual, user_tiles)
    pick_user = (tile_user[:, None] == jnp.arange(user_bf.shape[0], dtype=jnp.int32)[None, :]).astype(jnp.float32)
    pick_item = (tile_item[:, None] == jnp.arange(item_bf.shape[0], dtype=jnp.int32)[None, :]).astype(jnp.float32)
    grad_users = jnp.einsum('tn,tik->nik', pick_user, user_terms, precision=lax.Precision.HIGHEST).reshape(-1, width) + DECAY * users
    grad_items = jnp.einsum('tn,tik->nik', pick_item, item_terms, precision=lax.Precision.HIGHEST).reshape(-1, width) + DECAY * items
    user_accum = user_accum + grad_users * grad_users
    item_accum = item_accum + grad_items * grad_items
    users = users - LEARN_RATE * grad_users / jnp.sqrt(user_accum)
    items = items - LEARN_RATE * grad_items / jnp.sqrt(item_accum)
    return (users, user_accum, items, item_accum)

def reference(users, user_accum, items, item_accum, seen_user, seen_item, row_live, col_live, neg_user, neg_item):
    devices = N_BLK * N_XOR
    user_blocks = users.reshape(devices, USER_DEV, K)
    user_sums = user_accum.reshape(devices, USER_DEV, K)
    state = jnp.stack([items, item_accum]).reshape(2, N_BLK, N_XOR, 2, HALF, K)
    seen_u = seen_user.reshape(SUBS, devices, OBS)
    seen_i = seen_item.reshape(SUBS, devices, OBS)
    rows_l = row_live.reshape(SUBS, devices, OBS, TILE)
    cols_l = col_live.reshape(SUBS, devices, OBS, TILE)
    neg_u = neg_user.reshape(SUBS, devices, NEG)
    neg_i = neg_item.reshape(SUBS, devices, NEG)
    for sub_round in range(SUBS):
        flat = state.reshape(2, devices, ITEM_DEV, K)
        result = lax.map(lambda pack: local_step(*pack), (user_blocks, user_sums, flat[0], flat[1], seen_u[sub_round], seen_i[sub_round], rows_l[sub_round], cols_l[sub_round], neg_u[sub_round], neg_i[sub_round]))
        user_blocks, user_sums = (result[0], result[1])
        state = jnp.stack([result[2], result[3]]).reshape(2, N_BLK, N_XOR, 2, HALF, K)
        if sub_round + 1 < SUBS:
            state = jnp.roll(state, 1, axis=1)
            partner = np.arange(N_XOR) ^ 1 << sub_round % 2
            state = state.at[:, :, :, 1].set(state[:, :, partner, 1])
    flat = state.reshape(2, ITEMS, K)
    return (user_blocks.reshape(USERS, K), user_sums.reshape(USERS, K), flat[0], flat[1])
```

```python
import functools

import jax
import jax.numpy as jnp
from jax import lax
from jax.experimental import pallas as pl
from jax.experimental.pallas import tpu as pltpu
from jax.sharding import PartitionSpec as P

SUBS = 6
TILE = 128
LEARN_RATE = 0.05
DECAY = 0.02
NEG_WEIGHT = 0.25
MESH = pl.DeviceIdType.MESH
F32 = jnp.float32
BF16 = jnp.bfloat16


def flipped(index, bit):
    step = 2**bit
    return index + step - 2 * step * ((index // step) % 2)


def as_column(row):
    n = row.shape[1]
    full = jnp.broadcast_to(row, (n, n))
    diagonal = lax.broadcasted_iota(jnp.int32, (n, n), 0) == lax.broadcasted_iota(
        jnp.int32, (n, n), 1
    )
    return jnp.sum(jnp.where(diagonal, full, 0), axis=1, keepdims=True)


def one_hot_rows(column, live, tiles):
    return jnp.concatenate(
        [jnp.where(column == tile, live, 0.0) for tile in range(tiles)], axis=1
    )


def dot(a, b, ca, cb):
    return lax.dot_general(a, b, (((ca,), (cb,)), ((), ())), preferred_element_type=F32)


def kernel(
    n_blk,
    users_ref,
    user_accum_ref,
    items_ref,
    item_accum_ref,
    seen_user_ref,
    seen_item_ref,
    row_live_ref,
    col_live_ref,
    neg_user_ref,
    neg_item_ref,
    users_out,
    user_accum_out,
    items_out,
    item_accum_out,
    state,
    ub,
    vb,
    grad_users,
    grad_items,
    rows,
    cols,
    send_sem,
    recv_sem,
):
    blk = lax.axis_index("blk")
    xor = lax.axis_index("xor")
    ahead = lax.rem(blk + 1, n_blk)
    behind = lax.rem(blk + n_blk - 1, n_blk)

    barrier = pltpu.get_barrier_semaphore()
    for other in (xor, flipped(xor, 0), flipped(xor, 1)):
        pl.semaphore_signal(barrier, inc=1, device_id=(behind, other), device_id_type=MESH)

    n_users, width = users_ref.shape
    half = items_ref.shape[0] // 2
    block = 256
    n_obs = seen_user_ref.shape[1]
    n_neg = neg_user_ref.shape[1]
    pad = rows.shape[0] - n_obs - n_neg

    ub[...] = users_ref[...].astype(BF16)

    def masks(s):
        user_tiles, item_tiles = n_users // TILE, 2 * half // TILE
        root = jnp.full((n_neg, TILE), NEG_WEIGHT**0.5, F32)
        for index, negative, live, out, tiles in (
            (seen_user_ref, neg_user_ref, row_live_ref, rows, user_tiles),
            (seen_item_ref, neg_item_ref, col_live_ref, cols, item_tiles),
        ):
            observed = one_hot_rows(
                as_column(index[pl.ds(s, 1), :]), live[s].astype(F32), tiles
            )
            sampled = one_hot_rows(as_column(negative[pl.ds(s, 1), :]), root, tiles)
            out[...] = jnp.concatenate(
                [observed, sampled, jnp.zeros((pad, tiles * TILE), F32)], axis=0
            ).astype(BF16)

    def copy(s, h):
        to = xor if h == 0 else flipped(xor, s % 2)
        return pltpu.make_async_remote_copy(
            src_ref=state.at[s, h],
            dst_ref=state.at[s + 1, h],
            send_sem=send_sem.at[s, h],
            recv_sem=recv_sem.at[s, h],
            device_id=(ahead, to),
            device_id_type=MESH,
        )

    for s in range(SUBS):
        masks(s)
        for h in range(2):
            if s > 0:
                copy(s - 1, h).wait_recv()
            here = pl.ds(h * half, half)
            if s == 0:
                factor, accum = items_ref.at[here], item_accum_ref.at[here]
            else:
                factor, accum = state.at[s, h, 0], state.at[s, h, 1]
            if s == SUBS - 1:
                new_factor, new_accum = items_out.at[here], item_accum_out.at[here]
            else:
                new_factor, new_accum = state.at[s, h, 0], state.at[s, h, 1]
            vb[...] = factor[...].astype(BF16)
            grad_items[...] = DECAY * factor[...]

            def terms(u, carry, h=h):
                span = pl.ds(pl.multiple_of(u * block, block), block)
                here = pl.ds(h * half, half)
                scores = dot(ub[span], vb[...], 1, 1)
                weight = dot(rows[:, span], cols[:, here], 0, 0)
                seen = dot(rows[:n_obs, span], cols[:n_obs, here], 0, 0)
                err = (weight * scores - seen).astype(BF16)
                user_terms = dot(err, vb[...], 1, 0)
                if h == 0:
                    grad_users[span] = user_terms
                else:
                    grad_users[span] += user_terms
                grad_items[...] += dot(err, ub[span], 0, 0)
                return carry

            lax.fori_loop(0, n_users // block, terms, 0)

            grad = grad_items[...]
            summed = accum[...] + grad * grad
            new_accum[...] = summed
            new_factor[...] = factor[...] - LEARN_RATE * grad * lax.rsqrt(summed)
            if s < SUBS - 1:
                if s == 0 and h == 0:
                    pl.semaphore_wait(barrier, 3)
                copy(s, h).start()

        old, old_accum = (
            (users_ref, user_accum_ref) if s == 0 else (users_out, user_accum_out)
        )

        def update(u, carry, old=old, old_accum=old_accum):
            span = pl.ds(pl.multiple_of(u * block, block), block)
            now = old[span]
            grad = grad_users[span] + DECAY * now
            summed = old_accum[span] + grad * grad
            user_accum_out[span] = summed
            now = now - LEARN_RATE * grad * lax.rsqrt(summed)
            users_out[span] = now
            ub[span] = now.astype(BF16)
            return carry

        lax.fori_loop(0, n_users // block, update, 0)

    for s in range(SUBS - 1):
        for h in range(2):
            copy(s, h).wait_send()


def per_device(n_blk, *args):
    users, _, items = args[:3]
    n_users, width = users.shape
    n_items = items.shape[0]
    half = n_items // 2
    entries = -(-(args[4].shape[1] + args[8].shape[1]) // 16) * 16
    vmem = pl.BlockSpec(memory_space=pltpu.VMEM)
    flops = SUBS * 2 * 3 * n_users * n_items * width
    return pl.pallas_call(
        functools.partial(kernel, n_blk),
        out_shape=(
            jax.ShapeDtypeStruct(users.shape, F32),
            jax.ShapeDtypeStruct(users.shape, F32),
            jax.ShapeDtypeStruct(items.shape, F32),
            jax.ShapeDtypeStruct(items.shape, F32),
        ),
        in_specs=[vmem] * 10,
        out_specs=(vmem,) * 4,
        scratch_shapes=[
            pltpu.VMEM((SUBS, 2, 2, half, width), F32),
            pltpu.VMEM((n_users, width), BF16),
            pltpu.VMEM((half, width), BF16),
            pltpu.VMEM((n_users, width), F32),
            pltpu.VMEM((half, width), F32),
            pltpu.VMEM((entries, n_users), BF16),
            pltpu.VMEM((entries, n_items), BF16),
            pltpu.SemaphoreType.DMA((SUBS - 1, 2)),
            pltpu.SemaphoreType.DMA((SUBS - 1, 2)),
        ],
        compiler_params=pltpu.CompilerParams(
            collective_id=0, has_side_effects=True, vmem_limit_bytes=40 * 2**20
        ),
        cost_estimate=pl.CostEstimate(
            flops=flops, bytes_accessed=12 * 2**20, transcendentals=0
        ),
    )(*args)


def solution(mesh):
    flat = P(("blk", "xor"), None)
    tiles = P(None, ("blk", "xor"))
    live = P(None, ("blk", "xor"), None)
    return jax.shard_map(
        functools.partial(per_device, mesh.shape["blk"]),
        mesh=mesh,
        in_specs=(flat, flat, flat, flat, tiles, tiles, live, live, tiles, tiles),
        out_specs=(flat, flat, flat, flat),
        check_vma=False,
    )
```

```python
import functools

import jax
import jax.numpy as jnp
from jax import lax
from jax.experimental import pallas as pl
from jax.experimental.pallas import tpu as pltpu
from jax.sharding import PartitionSpec as P

SUBS = 6
TILE = 128
LEARN_RATE = 0.05
DECAY = 0.02
NEG_WEIGHT = 0.25
MESH = pl.DeviceIdType.MESH
F32 = jnp.float32
BF16 = jnp.bfloat16


def flipped(index, bit):
    step = 2**bit
    return index + step - 2 * step * ((index // step) % 2)


def as_column(row):
    n = row.shape[1]
    full = jnp.broadcast_to(row, (n, n))
    diagonal = lax.broadcasted_iota(jnp.int32, (n, n), 0) == lax.broadcasted_iota(
        jnp.int32, (n, n), 1
    )
    return jnp.sum(jnp.where(diagonal, full, 0), axis=1, keepdims=True)


def one_hot_rows(column, live, tiles):
    return jnp.concatenate(
        [jnp.where(column == tile, live, 0.0) for tile in range(tiles)], axis=1
    )


def dot(a, b, ca, cb):
    return lax.dot_general(a, b, (((ca,), (cb,)), ((), ())), preferred_element_type=F32)


def kernel(
    n_blk,
    users_in,
    user_accum_in,
    items_in,
    item_accum_in,
    seen_user_in,
    seen_item_in,
    row_live_in,
    col_live_in,
    neg_user_in,
    neg_item_in,
    users_out,
    user_accum_out,
    items_out,
    item_accum_out,
    state,
    lent,
    made,
    given,
    ub,
    vb,
    grad_users,
    grad_items,
    rows,
    cols,
    seen_user_ref,
    seen_item_ref,
    row_live_ref,
    col_live_ref,
    neg_user_ref,
    neg_item_ref,
    send_sem,
    recv_sem,
    load_sem,
):
    blk = lax.axis_index("blk")
    xor = lax.axis_index("xor")
    parity = lax.rem(blk, 2)

    def at(by):
        return lax.rem(blk + n_blk + by, n_blk)

    swap0, swap1 = flipped(xor, 0), flipped(xor, 1)
    swap01 = flipped(swap0, 1)
    barrier = pltpu.get_barrier_semaphore()

    def greet(by, others):
        for other in others:
            pl.semaphore_signal(
                barrier, inc=1, device_id=(at(by), other), device_id_type=MESH
            )

    greet(-2, (xor, swap01))
    greet(-1, (xor, swap0, swap1))

    @pl.when(parity == 0)
    def _():
        greet(1, (xor, swap1))

    n_users, width = users_in.shape
    half = items_in.shape[0] // 2
    block = 256
    n_obs = seen_user_ref.shape[1]
    n_neg = neg_user_ref.shape[1]
    pad = rows.shape[0] - n_obs - n_neg

    halves = [pl.ds(h * half, half) for h in range(2)]
    pairs = (
        (users_in, users_out),
        (items_in.at[halves[0]], state.at[0, 0, 0]),
        (seen_user_in, seen_user_ref),
        (seen_item_in, seen_item_ref),
        (row_live_in, row_live_ref),
        (col_live_in, col_live_ref),
        (neg_user_in, neg_user_ref),
        (neg_item_in, neg_item_ref),
        (item_accum_in.at[halves[0]], state.at[0, 0, 1]),
        (items_in.at[halves[1]], state.at[0, 1, 0]),
        (item_accum_in.at[halves[1]], state.at[0, 1, 1]),
        (user_accum_in, user_accum_out),
    )
    loads = [
        pltpu.make_async_copy(source, target, load_sem.at[i])
        for i, (source, target) in enumerate(pairs)
    ]
    for load in loads:
        load.start()
    for load in loads[2:8]:
        load.wait()

    def masks(s):
        user_tiles, item_tiles = n_users // TILE, 2 * half // TILE
        root = jnp.full((n_neg, TILE), NEG_WEIGHT**0.5, F32)
        for index, negative, live, out, tiles in (
            (seen_user_ref, neg_user_ref, row_live_ref, rows, user_tiles),
            (seen_item_ref, neg_item_ref, col_live_ref, cols, item_tiles),
        ):
            observed = one_hot_rows(
                as_column(index[pl.ds(s, 1), :]), live[s].astype(F32), tiles
            )
            sampled = one_hot_rows(as_column(negative[pl.ds(s, 1), :]), root, tiles)
            out[...] = jnp.concatenate(
                [observed, sampled, jnp.zeros((pad, tiles * TILE), F32)], axis=0
            ).astype(BF16)

    def remote(source, target, kind, c, h, device):
        return pltpu.make_async_remote_copy(
            src_ref=source,
            dst_ref=target,
            send_sem=send_sem.at[c, kind, h],
            recv_sem=recv_sem.at[c, kind, h],
            device_id=device,
            device_id_type=MESH,
        )

    def factor_on(c, h):
        to = (at(2), xor if h == 0 else swap01)
        return remote(state.at[c, h, 0], state.at[c + 1, h, 0], 0, c, h, to)

    def accum_on(c, h):
        to = (at(2), xor if h == 0 else swap01)
        return remote(state.at[c, h, 1], state.at[c + 1, h, 1], 1, c, h, to)

    def lend(c, h):
        to = (at(1), xor if h == 0 else swap0)
        return remote(state.at[c, h, 0], lent.at[c, h], 2, c, h, to)

    def lend_back(c, h):
        to = (at(-1), xor if h == 0 else swap1)
        return remote(state.at[c + 1, h, 0], lent.at[c, h], 2, c, h, to)

    def give_grad(c, h):
        to = (at(1), xor if h == 0 else swap1)
        return remote(made.at[c, h], given.at[c, h], 3, c, h, to)

    def last_move(h):
        to = (at(1), xor if h == 0 else swap0)
        return remote(state.at[2, h], state.at[3, h], 0, 2, h, to)

    def work(h, factor, grad):
        vb[...] = factor[...].astype(BF16)
        grad[...] = DECAY * factor[...]

        def terms(u, carry):
            span = pl.ds(pl.multiple_of(u * block, block), block)
            scores = dot(ub[span], vb[...], 1, 1)
            weight = dot(rows[:, span], cols[:, halves[h]], 0, 0)
            seen = dot(rows[:n_obs, span], cols[:n_obs, halves[h]], 0, 0)
            err = (weight * scores - seen).astype(BF16)
            user_terms = dot(err, vb[...], 1, 0)
            if h == 0:
                grad_users[span] = user_terms
            else:
                grad_users[span] += user_terms
            grad[...] += dot(err, ub[span], 0, 0)
            return carry

        lax.fori_loop(0, n_users // block, terms, 0)

    def adagrad(factor, accum, grad_ref, new_factor, new_accum):
        grad = grad_ref[...]
        summed = accum[...] + grad * grad
        new_accum[...] = summed
        new_factor[...] = factor[...] - LEARN_RATE * grad * lax.rsqrt(summed)

    def update_users():
        def update(u, carry):
            span = pl.ds(pl.multiple_of(u * block, block), block)
            now = users_out[span]
            grad = grad_users[span] + DECAY * now
            summed = user_accum_out[span] + grad * grad
            user_accum_out[span] = summed
            now = now - LEARN_RATE * grad * lax.rsqrt(summed)
            users_out[span] = now
            ub[span] = now.astype(BF16)
            return carry

        lax.fori_loop(0, n_users // block, update, 0)

    cycles = SUBS // 2 - 1
    for c in range(cycles + 1):
        masks(2 * c)
        if c == 0:
            loads[0].wait()
            ub[...] = users_out[...].astype(BF16)
        for h in range(2):
            factor, accum = state.at[c, h, 0], state.at[c, h, 1]
            if c == 0:
                loads[1 if h == 0 else 9].wait()
            else:
                accum_on(c - 1, h).wait_recv()
                lend(c - 1, h).wait_send()
                give_grad(c - 1, h).wait_recv()
                adagrad(factor, accum, given.at[c - 1, h], factor, accum)
            work(h, factor, grad_items)
            if c == 0:
                loads[8 if h == 0 else 10].wait()
            adagrad(factor, accum, grad_items, factor, accum)
            if c == 0 and h == 0:
                pl.semaphore_wait(barrier, 5 + 2 * parity)
            if c == cycles:
                last_move(h).start()
            else:

                @pl.when(parity == 0)
                def _(c=c, h=h):
                    lend(c, h).start()

                factor_on(c, h).start()
        if c < cycles:
            accum_on(c, 0).start()
            accum_on(c, 1).start()
        if c == 0:
            loads[11].wait()
        update_users()
        if c == cycles:
            break

        masks(2 * c + 1)
        for h in range(2):
            factor_on(c, h).wait_recv()

            @pl.when(parity == 1)
            def _(c=c, h=h):
                lend_back(c, h).start()

            lend(c, h).wait_recv()
            work(h, lent.at[c, h], made.at[c, h])
            give_grad(c, h).start()
        update_users()

    masks(SUBS - 1)
    for h in range(2):
        last_move(h).wait_recv()
        factor, accum = state.at[cycles + 1, h, 0], state.at[cycles + 1, h, 1]
        work(h, factor, grad_items)
        here = halves[h]
        adagrad(factor, accum, grad_items, items_out.at[here], item_accum_out.at[here])
    update_users()

    for h in range(2):
        for c in range(cycles):
            factor_on(c, h).wait_send()
            accum_on(c, h).wait_send()
            give_grad(c, h).wait_send()
        last_move(h).wait_send()


def per_device(n_blk, *args):
    users, _, items = args[:3]
    n_users, width = users.shape
    n_items = items.shape[0]
    half = n_items // 2
    entries = -(-(args[4].shape[1] + args[8].shape[1]) // 16) * 16
    vmem = pl.BlockSpec(memory_space=pltpu.VMEM)
    flops = SUBS * 2 * 3 * n_users * n_items * width
    return pl.pallas_call(
        functools.partial(kernel, n_blk),
        out_shape=(
            jax.ShapeDtypeStruct(users.shape, F32),
            jax.ShapeDtypeStruct(users.shape, F32),
            jax.ShapeDtypeStruct(items.shape, F32),
            jax.ShapeDtypeStruct(items.shape, F32),
        ),
        in_specs=[pl.BlockSpec(memory_space=pl.ANY)] * 10,
        out_specs=(vmem,) * 4,
        scratch_shapes=[
            pltpu.VMEM((SUBS // 2 + 1, 2, 2, half, width), F32),
            *[pltpu.VMEM((SUBS // 2 - 1, 2, half, width), F32)] * 3,
            pltpu.VMEM((n_users, width), BF16),
            pltpu.VMEM((half, width), BF16),
            pltpu.VMEM((n_users, width), F32),
            pltpu.VMEM((half, width), F32),
            pltpu.VMEM((entries, n_users), BF16),
            pltpu.VMEM((entries, n_items), BF16),
            *[pltpu.VMEM(arg.shape, arg.dtype) for arg in args[4:]],
            pltpu.SemaphoreType.DMA((SUBS // 2, 4, 2)),
            pltpu.SemaphoreType.DMA((SUBS // 2, 4, 2)),
            pltpu.SemaphoreType.DMA((12,)),
        ],
        compiler_params=pltpu.CompilerParams(
            collective_id=0, has_side_effects=True, vmem_limit_bytes=56 * 2**20
        ),
        cost_estimate=pl.CostEstimate(
            flops=flops, bytes_accessed=12 * 2**20, transcendentals=0
        ),
    )(*args)


def solution(mesh):
    flat = P(("blk", "xor"), None)
    tiles = P(None, ("blk", "xor"))
    live = P(None, ("blk", "xor"), None)
    return jax.shard_map(
        functools.partial(per_device, mesh.shape["blk"]),
        mesh=mesh,
        in_specs=(flat, flat, flat, flat, tiles, tiles, live, live, tiles, tiles),
        out_specs=(flat, flat, flat, flat),
        check_vma=False,
    )
```

```python
import functools

import jax
import jax.numpy as jnp
from jax import lax
from jax.experimental import pallas as pl
from jax.experimental.pallas import tpu as pltpu
from jax.sharding import PartitionSpec as P

SUBS = 6
TILE = 128
LEARN_RATE = 0.05
DECAY = 0.02
NEG_WEIGHT = 0.25
PARTS = 2
MESH = pl.DeviceIdType.MESH
F32 = jnp.float32
BF16 = jnp.bfloat16


def flipped(index, bit):
    step = 2**bit
    return index + step - 2 * step * ((index // step) % 2)


def as_column(row):
    n = row.shape[1]
    full = jnp.broadcast_to(row, (n, n))
    diagonal = lax.broadcasted_iota(jnp.int32, (n, n), 0) == lax.broadcasted_iota(
        jnp.int32, (n, n), 1
    )
    return jnp.sum(jnp.where(diagonal, full, 0), axis=1, keepdims=True)


def one_hot_rows(column, live, tiles):
    return jnp.concatenate(
        [jnp.where(column == tile, live, 0.0) for tile in range(tiles)], axis=1
    )


def dot(a, b, ca, cb):
    return lax.dot_general(a, b, (((ca,), (cb,)), ((), ())), preferred_element_type=F32)


def kernel(
    n_blk,
    users_in,
    user_accum_in,
    items_in,
    item_accum_in,
    seen_user_in,
    seen_item_in,
    row_live_in,
    col_live_in,
    neg_user_in,
    neg_item_in,
    users_out,
    user_accum_out,
    items_out,
    item_accum_out,
    state,
    lent,
    made,
    given,
    ub,
    vb,
    grad_users,
    grad_items,
    rows,
    cols,
    seen_user_ref,
    seen_item_ref,
    row_live_ref,
    col_live_ref,
    neg_user_ref,
    neg_item_ref,
    send_sem,
    recv_sem,
    load_sem,
):
    blk = lax.axis_index("blk")
    xor = lax.axis_index("xor")
    parity = lax.rem(blk, 2)

    def at(by):
        return lax.rem(blk + n_blk + by, n_blk)

    swap0, swap1 = flipped(xor, 0), flipped(xor, 1)
    swap01 = flipped(swap0, 1)
    barrier = pltpu.get_barrier_semaphore()

    def greet(by, others):
        for other in others:
            pl.semaphore_signal(
                barrier, inc=1, device_id=(at(by), other), device_id_type=MESH
            )

    greet(-2, (xor, swap01))
    greet(-1, (xor, swap0, swap1))

    @pl.when(parity == 0)
    def _():
        greet(1, (xor, swap1))

    n_users, width = users_in.shape
    half = items_in.shape[0] // 2
    block = 256
    n_obs = seen_user_ref.shape[1]
    n_neg = neg_user_ref.shape[1]
    pad = rows.shape[0] - n_obs - n_neg

    halves = [pl.ds(h * half, half) for h in range(2)]
    pairs = (
        (users_in, users_out),
        (items_in.at[halves[0]], state.at[0, 0, 0]),
        (seen_user_in, seen_user_ref),
        (seen_item_in, seen_item_ref),
        (row_live_in, row_live_ref),
        (col_live_in, col_live_ref),
        (neg_user_in, neg_user_ref),
        (neg_item_in, neg_item_ref),
        (item_accum_in.at[halves[0]], state.at[0, 0, 1]),
        (items_in.at[halves[1]], state.at[0, 1, 0]),
        (item_accum_in.at[halves[1]], state.at[0, 1, 1]),
        (user_accum_in, user_accum_out),
    )
    loads = [
        pltpu.make_async_copy(source, target, load_sem.at[i])
        for i, (source, target) in enumerate(pairs)
    ]
    for load in loads:
        load.start()
    for load in loads[2:8]:
        load.wait()

    def masks(s):
        user_tiles, item_tiles = n_users // TILE, 2 * half // TILE
        root = jnp.full((n_neg, TILE), NEG_WEIGHT**0.5, F32)
        for index, negative, live, out, tiles in (
            (seen_user_ref, neg_user_ref, row_live_ref, rows, user_tiles),
            (seen_item_ref, neg_item_ref, col_live_ref, cols, item_tiles),
        ):
            observed = one_hot_rows(
                as_column(index[pl.ds(s, 1), :]), live[s].astype(F32), tiles
            )
            sampled = one_hot_rows(as_column(negative[pl.ds(s, 1), :]), root, tiles)
            out[...] = jnp.concatenate(
                [observed, sampled, jnp.zeros((pad, tiles * TILE), F32)], axis=0
            ).astype(BF16)

    def remote(source, target, kind, c, h, device):
        return pltpu.make_async_remote_copy(
            src_ref=source,
            dst_ref=target,
            send_sem=send_sem.at[c, kind, h],
            recv_sem=recv_sem.at[c, kind, h],
            device_id=device,
            device_id_type=MESH,
        )

    def factor_on(c, h):
        to = (at(2), xor if h == 0 else swap01)
        return remote(state.at[c, h, 0], state.at[c + 1, h, 0], 0, c, h, to)

    def accum_on(c, h):
        to = (at(2), xor if h == 0 else swap01)
        return remote(state.at[c, h, 1], state.at[c + 1, h, 1], 1, c, h, to)

    def lend(c, h):
        to = (at(1), xor if h == 0 else swap0)
        return remote(state.at[c, h, 0], lent.at[c, h], 2, c, h, to)

    def lend_back(c, h):
        to = (at(-1), xor if h == 0 else swap1)
        return remote(state.at[c + 1, h, 0], lent.at[c, h], 2, c, h, to)

    def give_grad(c, h):
        to = (at(1), xor if h == 0 else swap1)
        return remote(made.at[c, h], given.at[c, h], 3, c, h, to)

    def last_move(h):
        to = (at(1), xor if h == 0 else swap0)
        return remote(state.at[2, h], state.at[3, h], 0, 2, h, to)

    def work(h, factor, grad):
        vb[...] = factor[...].astype(BF16)
        grad[...] = DECAY * factor[...]

        def terms(u, carry):
            span = pl.ds(pl.multiple_of(u * block, block), block)
            scores = dot(ub[span], vb[...], 1, 1)
            weight = dot(rows[:, span], cols[:, halves[h]], 0, 0)
            seen = dot(rows[:n_obs, span], cols[:n_obs, halves[h]], 0, 0)
            err = (weight * scores - seen).astype(BF16)
            user_terms = dot(err, vb[...], 1, 0)
            if h == 0:
                grad_users[span] = user_terms
            else:
                grad_users[span] += user_terms
            grad[...] += dot(err, ub[span], 0, 0)
            return carry

        lax.fori_loop(0, n_users // block, terms, 0)

    def adagrad(factor, accum, grad_ref, new_factor, new_accum):
        grad = grad_ref[...]
        summed = accum[...] + grad * grad
        new_accum[...] = summed
        new_factor[...] = factor[...] - LEARN_RATE * grad * lax.rsqrt(summed)

    def update_users():
        def update(u, carry):
            span = pl.ds(pl.multiple_of(u * block, block), block)
            now = users_out[span]
            grad = grad_users[span] + DECAY * now
            summed = user_accum_out[span] + grad * grad
            user_accum_out[span] = summed
            now = now - LEARN_RATE * grad * lax.rsqrt(summed)
            users_out[span] = now
            ub[span] = now.astype(BF16)
            return carry

        lax.fori_loop(0, n_users // block, update, 0)

    cycles = SUBS // 2 - 1
    for c in range(cycles + 1):
        masks(2 * c)
        if c == 0:
            loads[0].wait()
            ub[...] = users_out[...].astype(BF16)
        for h in range(2):
            factor, accum = state.at[c, h, 0], state.at[c, h, 1]
            if c == 0:
                loads[1 if h == 0 else 9].wait()
            else:
                accum_on(c - 1, h).wait_recv()
                lend(c - 1, h).wait_send()
                give_grad(c - 1, h).wait_recv()
                adagrad(factor, accum, given.at[c - 1, h], factor, accum)
            work(h, factor, grad_items)
            if c == 0:
                loads[8 if h == 0 else 10].wait()
            adagrad(factor, accum, grad_items, factor, accum)
            if c == 0 and h == 0:
                pl.semaphore_wait(barrier, 5 + 2 * parity)
            if c == cycles:
                last_move(h).start()
            else:

                @pl.when(parity == 0)
                def _(c=c, h=h):
                    lend(c, h).start()

                factor_on(c, h).start()
        if c == 0:
            loads[11].wait()
        update_users()
        if c == cycles:
            break

        masks(2 * c + 1)
        for h in range(2):
            factor_on(c, h).wait_recv()

            @pl.when(parity == 1)
            def _(c=c, h=h):
                lend_back(c, h).start()

            lend(c, h).wait_recv()
            work(h, lent.at[c, h], made.at[c, h])
            give_grad(c, h).start()
            if h == 0:
                for i in range(2):
                    factor_on(c, i).wait_send()
                for i in range(2):
                    accum_on(c, i).start()
        update_users()

    masks(SUBS - 1)
    for h in range(2):
        last_move(h).wait_recv()
        factor, accum = state.at[cycles + 1, h, 0], state.at[cycles + 1, h, 1]
        work(h, factor, grad_items)
        here = halves[h]
        adagrad(factor, accum, grad_items, items_out.at[here], item_accum_out.at[here])
    update_users()

    for h in range(2):
        for c in range(cycles):
            accum_on(c, h).wait_send()
            give_grad(c, h).wait_send()
        last_move(h).wait_send()


def write_out(*refs):
    sources, targets, sems = refs[:4], refs[4:8], refs[8]
    copies = []
    for i, (source, target) in enumerate(zip(sources, targets)):
        n = source.shape[0] // PARTS
        for part in range(PARTS):
            span = pl.ds(part * n, n)
            copies.append(
                pltpu.make_async_copy(source.at[span], target.at[span], sems.at[i, part])
            )
    for copy in copies:
        copy.start()
    for copy in copies:
        copy.wait()


def per_device(n_blk, *args):
    users, _, items = args[:3]
    n_users, width = users.shape
    n_items = items.shape[0]
    half = n_items // 2
    entries = -(-(args[4].shape[1] + args[8].shape[1]) // 16) * 16
    vmem = pl.BlockSpec(memory_space=pltpu.VMEM)
    flops = SUBS * 2 * 3 * n_users * n_items * width
    results = pl.pallas_call(
        functools.partial(kernel, n_blk),
        out_shape=(
            jax.ShapeDtypeStruct(users.shape, F32),
            jax.ShapeDtypeStruct(users.shape, F32),
            jax.ShapeDtypeStruct(items.shape, F32),
            jax.ShapeDtypeStruct(items.shape, F32),
        ),
        in_specs=[pl.BlockSpec(memory_space=pl.ANY)] * 10,
        out_specs=(vmem,) * 4,
        scratch_shapes=[
            pltpu.VMEM((SUBS // 2 + 1, 2, 2, half, width), F32),
            *[pltpu.VMEM((SUBS // 2 - 1, 2, half, width), F32)] * 3,
            pltpu.VMEM((n_users, width), BF16),
            pltpu.VMEM((half, width), BF16),
            pltpu.VMEM((n_users, width), F32),
            pltpu.VMEM((half, width), F32),
            pltpu.VMEM((entries, n_users), BF16),
            pltpu.VMEM((entries, n_items), BF16),
            *[pltpu.VMEM(arg.shape, arg.dtype) for arg in args[4:]],
            pltpu.SemaphoreType.DMA((SUBS // 2, 4, 2)),
            pltpu.SemaphoreType.DMA((SUBS // 2, 4, 2)),
            pltpu.SemaphoreType.DMA((12,)),
        ],
        compiler_params=pltpu.CompilerParams(
            collective_id=0, has_side_effects=True, vmem_limit_bytes=56 * 2**20
        ),
        cost_estimate=pl.CostEstimate(
            flops=flops, bytes_accessed=12 * 2**20, transcendentals=0
        ),
    )(*args)
    anywhere = pl.BlockSpec(memory_space=pl.ANY)
    return pl.pallas_call(
        write_out,
        out_shape=[jax.ShapeDtypeStruct(x.shape, x.dtype) for x in results],
        in_specs=[anywhere] * 4,
        out_specs=[anywhere] * 4,
        scratch_shapes=[pltpu.SemaphoreType.DMA((4, PARTS))],
        compiler_params=pltpu.CompilerParams(vmem_limit_bytes=56 * 2**20),
        cost_estimate=pl.CostEstimate(
            flops=0, bytes_accessed=6 * 2**20, transcendentals=0
        ),
    )(*results)


def solution(mesh):
    flat = P(("blk", "xor"), None)
    tiles = P(None, ("blk", "xor"))
    live = P(None, ("blk", "xor"), None)
    return jax.shard_map(
        functools.partial(per_device, mesh.shape["blk"]),
        mesh=mesh,
        in_specs=(flat, flat, flat, flat, tiles, tiles, live, live, tiles, tiles),
        out_specs=(flat, flat, flat, flat),
        check_vma=False,
    )
```

```python
import functools

import jax
import jax.numpy as jnp
from jax import lax
from jax.experimental import pallas as pl
from jax.experimental.pallas import tpu as pltpu
from jax.sharding import PartitionSpec as P

SUBS = 6
TILE = 128
LEARN_RATE = 0.05
DECAY = 0.02
NEG_WEIGHT = 0.25
PARTS = 2
MESH = pl.DeviceIdType.MESH
F32 = jnp.float32
BF16 = jnp.bfloat16


def flipped(index, bit):
    step = 2**bit
    return index + step - 2 * step * ((index // step) % 2)


def as_column(row):
    n = row.shape[1]
    full = jnp.broadcast_to(row, (n, n))
    diagonal = lax.broadcasted_iota(jnp.int32, (n, n), 0) == lax.broadcasted_iota(
        jnp.int32, (n, n), 1
    )
    return jnp.sum(jnp.where(diagonal, full, 0), axis=1, keepdims=True)


def one_hot_rows(column, live, tiles):
    return jnp.concatenate(
        [jnp.where(column == tile, live, 0.0) for tile in range(tiles)], axis=1
    )


def dot(a, b, ca, cb):
    return lax.dot_general(a, b, (((ca,), (cb,)), ((), ())), preferred_element_type=F32)


def kernel(
    n_blk,
    users_in,
    user_accum_in,
    items_in,
    item_accum_in,
    seen_user_in,
    seen_item_in,
    row_live_in,
    col_live_in,
    neg_user_in,
    neg_item_in,
    users_out,
    user_accum_out,
    items_out,
    item_accum_out,
    users,
    user_accum,
    state,
    lent,
    made,
    given,
    ub,
    vb,
    grad_users,
    grad_items,
    rows,
    cols,
    weight,
    seen,
    seen_user_ref,
    seen_item_ref,
    row_live_ref,
    col_live_ref,
    neg_user_ref,
    neg_item_ref,
    send_sem,
    recv_sem,
    load_sem,
    store_sem,
):
    blk = lax.axis_index("blk")
    xor = lax.axis_index("xor")
    parity = lax.rem(blk, 2)

    def at(by):
        return lax.rem(blk + n_blk + by, n_blk)

    swap0, swap1 = flipped(xor, 0), flipped(xor, 1)
    swap01 = flipped(swap0, 1)
    barrier = pltpu.get_barrier_semaphore()

    def greet(by, others):
        for other in others:
            pl.semaphore_signal(
                barrier, inc=1, device_id=(at(by), other), device_id_type=MESH
            )

    greet(-2, (xor, swap01))
    greet(-1, (xor, swap0, swap1))

    @pl.when(parity == 0)
    def _():
        greet(1, (xor, swap1))

    n_users, width = users_in.shape
    half = items_in.shape[0] // 2
    block = 256
    n_obs = seen_user_ref.shape[1]
    n_neg = neg_user_ref.shape[1]
    pad = rows.shape[0] - n_obs - n_neg

    halves = [pl.ds(h * half, half) for h in range(2)]
    pairs = (
        (users_in, users),
        (items_in.at[halves[0]], state.at[0, 0, 0]),
        (seen_user_in, seen_user_ref),
        (seen_item_in, seen_item_ref),
        (row_live_in, row_live_ref),
        (col_live_in, col_live_ref),
        (neg_user_in, neg_user_ref),
        (neg_item_in, neg_item_ref),
        (item_accum_in.at[halves[0]], state.at[0, 0, 1]),
        (items_in.at[halves[1]], state.at[0, 1, 0]),
        (item_accum_in.at[halves[1]], state.at[0, 1, 1]),
        (user_accum_in, user_accum),
    )
    loads = [
        pltpu.make_async_copy(source, target, load_sem.at[i])
        for i, (source, target) in enumerate(pairs)
    ]
    for load in loads:
        load.start()
    for load in loads[2:8]:
        load.wait()

    def masks(s):
        user_tiles, item_tiles = n_users // TILE, 2 * half // TILE
        root = jnp.full((n_neg, TILE), NEG_WEIGHT**0.5, F32)
        for index, negative, live, out, tiles in (
            (seen_user_ref, neg_user_ref, row_live_ref, rows, user_tiles),
            (seen_item_ref, neg_item_ref, col_live_ref, cols, item_tiles),
        ):
            observed = one_hot_rows(
                as_column(index[pl.ds(s, 1), :]), live[s].astype(F32), tiles
            )
            sampled = one_hot_rows(as_column(negative[pl.ds(s, 1), :]), root, tiles)
            out[...] = jnp.concatenate(
                [observed, sampled, jnp.zeros((pad, tiles * TILE), F32)], axis=0
            ).astype(BF16)

        def spread(u, carry):
            span = pl.ds(pl.multiple_of(u * block, block), block)
            weight[span] = dot(rows[:, span], cols[...], 0, 0).astype(BF16)
            seen[span] = dot(rows[:n_obs, span], cols[:n_obs], 0, 0).astype(BF16)
            return carry

        lax.fori_loop(0, n_users // block, spread, 0)

    def remote(source, target, kind, c, h, device, part=0):
        return pltpu.make_async_remote_copy(
            src_ref=source,
            dst_ref=target,
            send_sem=send_sem.at[c, kind, h, part],
            recv_sem=recv_sem.at[c, kind, h, part],
            device_id=device,
            device_id_type=MESH,
        )

    spans = [pl.ds(i * (half // PARTS), half // PARTS) for i in range(PARTS)]

    def factor_on(c, h, i):
        to = (at(2), xor if h == 0 else swap01)
        source, target = state.at[c, h, 0, spans[i]], state.at[c + 1, h, 0, spans[i]]
        return remote(source, target, 0, c, h, to, i)

    def accum_on(c, h):
        to = (at(2), xor if h == 0 else swap01)
        return remote(state.at[c, h, 1], state.at[c + 1, h, 1], 1, c, h, to)

    def lend(c, h, i):
        to = (at(1), xor if h == 0 else swap0)
        source, target = state.at[c, h, 0, spans[i]], lent.at[c, h, spans[i]]
        return remote(source, target, 2, c, h, to, i)

    def lend_back(c, h, i):
        to = (at(-1), xor if h == 0 else swap1)
        source, target = state.at[c + 1, h, 0, spans[i]], lent.at[c, h, spans[i]]
        return remote(source, target, 2, c, h, to, i)

    def give_grad(c, h):
        to = (at(1), xor if h == 0 else swap1)
        return remote(made.at[c, h], given.at[c, h], 3, c, h, to)

    def last_move(h, kind):
        to = (at(1), xor if h == 0 else swap0)
        return remote(state.at[2, h, kind], state.at[3, h, kind], kind, 2, h, to)

    def work(h, factor, grad):
        vb[...] = factor[...].astype(BF16)
        grad[...] = DECAY * factor[...]

        def terms(u, carry):
            span = pl.ds(pl.multiple_of(u * block, block), block)
            scores = dot(ub[span], vb[...], 1, 1)
            weighted = weight[span, halves[h]].astype(F32) * scores
            err = (weighted - seen[span, halves[h]].astype(F32)).astype(BF16)
            user_terms = dot(err, vb[...], 1, 0)
            if h == 0:
                grad_users[span] = user_terms
            else:
                grad_users[span] += user_terms
            grad[...] += dot(err, ub[span], 0, 0)
            return carry

        lax.fori_loop(0, n_users // block, terms, 0, unroll=True)

    def adagrad(factor, accum, grad_ref):
        grad = grad_ref[...]
        summed = accum[...] + grad * grad
        accum[...] = summed
        factor[...] = factor[...] - LEARN_RATE * grad * lax.rsqrt(summed)

    def update_users():
        def update(u, carry):
            span = pl.ds(pl.multiple_of(u * block, block), block)
            now = users[span]
            grad = grad_users[span] + DECAY * now
            summed = user_accum[span] + grad * grad
            user_accum[span] = summed
            now = now - LEARN_RATE * grad * lax.rsqrt(summed)
            users[span] = now
            ub[span] = now.astype(BF16)
            return carry

        lax.fori_loop(0, n_users // block, update, 0, unroll=True)

    cycles = SUBS // 2 - 1
    for c in range(cycles + 1):
        masks(2 * c)
        if c == 0:
            loads[0].wait()
            ub[...] = users[...].astype(BF16)
        for h in range(2):
            factor, accum = state.at[c, h, 0], state.at[c, h, 1]
            if c == 0:
                loads[1 if h == 0 else 9].wait()
            else:
                accum_on(c - 1, h).wait_recv()
                for i in range(PARTS):
                    lend(c - 1, h, i).wait_send()
                give_grad(c - 1, h).wait_recv()
                adagrad(factor, accum, given.at[c - 1, h])
            work(h, factor, grad_items.at[h])
            if c == 0:
                loads[8 if h == 0 else 10].wait()
            adagrad(factor, accum, grad_items.at[h])
            if c == 0 and h == 0:
                pl.semaphore_wait(barrier, 5 + 2 * parity)
            if c == cycles:
                last_move(h, 0).start()
            else:

                @pl.when(parity == 0)
                def _(c=c, h=h):
                    for i in range(PARTS):
                        lend(c, h, i).start()

                for i in range(PARTS):
                    factor_on(c, h, i).start()
        if c == 0:
            loads[11].wait()
        update_users()
        if c == cycles:
            break

        masks(2 * c + 1)
        for h in range(2):
            for i in range(PARTS):
                factor_on(c, h, i).wait_recv()

                @pl.when(parity == 1)
                def _(c=c, h=h, i=i):
                    lend_back(c, h, i).start()

            if h == 1:
                for k in range(2):
                    for i in range(PARTS):
                        factor_on(c, k, i).wait_send()
                for k in range(2):
                    accum_on(c, k).start()
            for i in range(PARTS):
                lend(c, h, i).wait_recv()
            work(h, lent.at[c, h], made.at[c, h])
            give_grad(c, h).start()
        update_users()

    masks(SUBS - 1)
    for h in range(2):
        last_move(h, 0).wait_send()
        last_move(h, 1).start()
        last_move(h, 0).wait_recv()
        work(h, state.at[cycles + 1, h, 0], grad_items.at[h])
    update_users()
    stores = [
        pltpu.make_async_copy(users, users_out, store_sem.at[0]),
        pltpu.make_async_copy(user_accum, user_accum_out, store_sem.at[1]),
    ]
    for store in stores:
        store.start()
    for h in range(2):
        last_move(h, 1).wait_recv()
        factor, accum = state.at[cycles + 1, h, 0], state.at[cycles + 1, h, 1]
        adagrad(factor, accum, grad_items.at[h])
        for i, (source, target) in enumerate(
            ((factor, items_out), (accum, item_accum_out))
        ):
            store = pltpu.make_async_copy(
                source, target.at[halves[h]], store_sem.at[2 + 2 * h + i]
            )
            store.start()
            stores.append(store)

    for h in range(2):
        for c in range(cycles):
            accum_on(c, h).wait_send()
            give_grad(c, h).wait_send()
        last_move(h, 1).wait_send()
    for store in stores:
        store.wait()


def write_out(*refs):
    sources, targets, buffers, (load_sem, store_sem) = (
        refs[:4],
        refs[4:8],
        refs[8:12],
        refs[12:],
    )
    loads, stores = [], []
    for i, (source, target, buffer) in enumerate(zip(sources, targets, buffers)):
        n = source.shape[0] // PARTS
        for part in range(PARTS):
            span = pl.ds(part * n, n)
            sems = load_sem.at[i, part], store_sem.at[i, part]
            loads.append(
                pltpu.make_async_copy(source.at[span], buffer.at[span], sems[0])
            )
            stores.append(
                pltpu.make_async_copy(buffer.at[span], target.at[span], sems[1])
            )
    for load in loads:
        load.start()
    for load, store in zip(loads, stores):
        load.wait()
        store.start()
    for store in stores:
        store.wait()


def per_device(n_blk, *args):
    users, _, items = args[:3]
    n_users, width = users.shape
    n_items = items.shape[0]
    half = n_items // 2
    entries = -(-(args[4].shape[1] + args[8].shape[1]) // 16) * 16
    anywhere = pl.BlockSpec(memory_space=pl.ANY)
    flops = SUBS * 2 * 3 * n_users * n_items * width
    results = pl.pallas_call(
        functools.partial(kernel, n_blk),
        out_shape=(
            jax.ShapeDtypeStruct(users.shape, F32),
            jax.ShapeDtypeStruct(users.shape, F32),
            jax.ShapeDtypeStruct(items.shape, F32),
            jax.ShapeDtypeStruct(items.shape, F32),
        ),
        in_specs=[anywhere] * 10,
        out_specs=(anywhere,) * 4,
        scratch_shapes=[
            pltpu.VMEM((n_users, width), F32),
            pltpu.VMEM((n_users, width), F32),
            pltpu.VMEM((SUBS // 2 + 1, 2, 2, half, width), F32),
            *[pltpu.VMEM((SUBS // 2 - 1, 2, half, width), F32)] * 3,
            pltpu.VMEM((n_users, width), BF16),
            pltpu.VMEM((half, width), BF16),
            pltpu.VMEM((n_users, width), F32),
            pltpu.VMEM((2, half, width), F32),
            pltpu.VMEM((entries, n_users), BF16),
            pltpu.VMEM((entries, n_items), BF16),
            pltpu.VMEM((n_users, n_items), BF16),
            pltpu.VMEM((n_users, n_items), BF16),
            *[pltpu.VMEM(arg.shape, arg.dtype) for arg in args[4:]],
            pltpu.SemaphoreType.DMA((SUBS // 2, 4, 2, PARTS)),
            pltpu.SemaphoreType.DMA((SUBS // 2, 4, 2, PARTS)),
            pltpu.SemaphoreType.DMA((12,)),
            pltpu.SemaphoreType.DMA((6,)),
        ],
        compiler_params=pltpu.CompilerParams(
            collective_id=0, has_side_effects=True, vmem_limit_bytes=56 * 2**20
        ),
        cost_estimate=pl.CostEstimate(
            flops=flops, bytes_accessed=12 * 2**20, transcendentals=0
        ),
    )(*args)
    return pl.pallas_call(
        write_out,
        out_shape=[jax.ShapeDtypeStruct(x.shape, x.dtype) for x in results],
        in_specs=[anywhere] * 4,
        out_specs=[anywhere] * 4,
        scratch_shapes=[
            *[pltpu.VMEM(x.shape, x.dtype) for x in results],
            pltpu.SemaphoreType.DMA((4, PARTS)),
            pltpu.SemaphoreType.DMA((4, PARTS)),
        ],
        compiler_params=pltpu.CompilerParams(vmem_limit_bytes=56 * 2**20),
        cost_estimate=pl.CostEstimate(
            flops=0, bytes_accessed=6 * 2**20, transcendentals=0
        ),
    )(*results)


def solution(mesh):
    flat = P(("blk", "xor"), None)
    tiles = P(None, ("blk", "xor"))
    live = P(None, ("blk", "xor"), None)
    return jax.shard_map(
        functools.partial(per_device, mesh.shape["blk"]),
        mesh=mesh,
        in_specs=(flat, flat, flat, flat, tiles, tiles, live, live, tiles, tiles),
        out_specs=(flat, flat, flat, flat),
        check_vma=False,
    )
```

```python
import functools

import jax
import jax.numpy as jnp
from jax import lax
from jax.experimental import pallas as pl
from jax.experimental.pallas import tpu as pltpu
from jax.sharding import PartitionSpec as P

SUBS = 6
TILE = 128
LEARN_RATE = 0.05
DECAY = 0.02
NEG_WEIGHT = 0.25
PARTS = 2
MESH = pl.DeviceIdType.MESH
F32 = jnp.float32
BF16 = jnp.bfloat16


def flipped(index, bit):
    step = 2**bit
    return index + step - 2 * step * ((index // step) % 2)


def as_column(row):
    n = row.shape[1]
    full = jnp.broadcast_to(row, (n, n))
    diagonal = lax.broadcasted_iota(jnp.int32, (n, n), 0) == lax.broadcasted_iota(
        jnp.int32, (n, n), 1
    )
    return jnp.sum(jnp.where(diagonal, full, 0), axis=1, keepdims=True)


def one_hot_rows(column, live, tiles):
    return jnp.concatenate(
        [jnp.where(column == tile, live, 0.0) for tile in range(tiles)], axis=1
    )


def dot(a, b, ca, cb):
    return lax.dot_general(a, b, (((ca,), (cb,)), ((), ())), preferred_element_type=F32)


def kernel(
    n_blk,
    users_in,
    user_accum_in,
    items_in,
    item_accum_in,
    seen_user_in,
    seen_item_in,
    row_live_in,
    col_live_in,
    neg_user_in,
    neg_item_in,
    users_out,
    user_accum_out,
    items_out,
    item_accum_out,
    users,
    user_accum,
    state,
    relay,
    ub,
    vb,
    grad_users,
    grad_items,
    rows,
    cols,
    weight,
    seen,
    seen_user_ref,
    seen_item_ref,
    row_live_ref,
    col_live_ref,
    neg_user_ref,
    neg_item_ref,
    send_sem,
    recv_sem,
    relay_send,
    relay_recv,
    load_sem,
    store_sem,
):
    blk = lax.axis_index("blk")
    xor = lax.axis_index("xor")
    parity = lax.rem(blk, 2)

    def at(by):
        return lax.rem(blk + n_blk + by, n_blk)

    swap0, swap1 = flipped(xor, 0), flipped(xor, 1)
    barrier = pltpu.get_barrier_semaphore()

    def greet(by, others):
        for other in others:
            pl.semaphore_signal(
                barrier, inc=1, device_id=(at(by), other), device_id_type=MESH
            )

    @pl.when(parity == 0)
    def _():
        greet(1, (xor, swap0, swap1))
        greet(-2, (xor, swap0, swap1))

    @pl.when(parity == 1)
    def _():
        greet(-1, (xor, swap0, swap1))
        greet(-2, (xor,))

    n_users, width = users_in.shape
    half = items_in.shape[0] // 2
    block = 256
    n_obs = seen_user_ref.shape[1]
    n_neg = neg_user_ref.shape[1]
    pad = rows.shape[0] - n_obs - n_neg

    halves = [pl.ds(h * half, half) for h in range(2)]
    size = half // PARTS
    pairs = [
        (users_in, users),
        (user_accum_in, user_accum),
        (seen_user_in, seen_user_ref),
        (seen_item_in, seen_item_ref),
        (row_live_in, row_live_ref),
        (col_live_in, col_live_ref),
        (neg_user_in, neg_user_ref),
        (neg_item_in, neg_item_ref),
    ]
    for h in range(2):
        for i in range(PARTS):
            from_rows = pl.ds(h * half + i * size, size)
            pairs.append((items_in.at[from_rows], state.at[0, h, i, 0]))
            pairs.append((item_accum_in.at[from_rows], state.at[0, h, i, 1]))
    loads = [
        pltpu.make_async_copy(source, target, load_sem.at[i])
        for i, (source, target) in enumerate(pairs)
    ]
    for load in loads:
        load.start()
    for load in loads[2:8]:
        load.wait()

    def masks(s):
        user_tiles, item_tiles = n_users // TILE, 2 * half // TILE
        root = jnp.full((n_neg, TILE), NEG_WEIGHT**0.5, F32)
        for index, negative, live, out, tiles in (
            (seen_user_ref, neg_user_ref, row_live_ref, rows, user_tiles),
            (seen_item_ref, neg_item_ref, col_live_ref, cols, item_tiles),
        ):
            observed = one_hot_rows(
                as_column(index[pl.ds(s, 1), :]), live[s].astype(F32), tiles
            )
            sampled = one_hot_rows(as_column(negative[pl.ds(s, 1), :]), root, tiles)
            out[...] = jnp.concatenate(
                [observed, sampled, jnp.zeros((pad, tiles * TILE), F32)], axis=0
            ).astype(BF16)

        def spread(u, carry):
            span = pl.ds(pl.multiple_of(u * block, block), block)
            weight[span] = dot(rows[:, span], cols[...], 0, 0).astype(BF16)
            seen[span] = dot(rows[:n_obs, span], cols[:n_obs], 0, 0).astype(BF16)
            return carry

        lax.fori_loop(0, n_users // block, spread, 0)

    def remote(source, target, sems, device):
        return pltpu.make_async_remote_copy(
            src_ref=source,
            dst_ref=target,
            send_sem=sems[0],
            recv_sem=sems[1],
            device_id=device,
            device_id_type=MESH,
        )

    def after(s, h):
        return xor if h == 0 else (swap0 if s % 2 == 0 else swap1)

    def direct(s, h, i):
        return remote(
            state.at[s, h, i],
            state.at[s + 1, h, i],
            (send_sem.at[s, h, i], recv_sem.at[s, h, i]),
            (at(1), after(s, h)),
        )

    def first_hop(s, h, i):
        return remote(
            state.at[s, h, i],
            relay.at[s, h],
            (send_sem.at[s, h, i], relay_recv.at[s, h]),
            (at(2) if i == 0 else at(-1), xor),
        )

    def second_hop(s, h, i):
        return remote(
            relay.at[s, h],
            state.at[s + 1, h, i],
            (relay_send.at[s, h], recv_sem.at[s, h, i]),
            (at(-1) if i == 0 else at(2), after(s, h)),
        )

    def work(h, slot):
        for i in range(PARTS):
            factor = state[slot, h, i, 0]
            vb[pl.ds(i * size, size)] = factor.astype(BF16)
            grad_items[pl.ds(i * size, size)] = DECAY * factor

        def terms(u, carry):
            span = pl.ds(pl.multiple_of(u * block, block), block)
            scores = dot(ub[span], vb[...], 1, 1)
            weighted = weight[span, halves[h]].astype(F32) * scores
            err = (weighted - seen[span, halves[h]].astype(F32)).astype(BF16)
            user_terms = dot(err, vb[...], 1, 0)
            if h == 0:
                grad_users[span] = user_terms
            else:
                grad_users[span] += user_terms
            grad_items[...] += dot(err, ub[span], 0, 0)
            return carry

        lax.fori_loop(0, n_users // block, terms, 0, unroll=True)

    def adagrad(slot, h, i):
        grad = grad_items[pl.ds(i * size, size)]
        summed = state[slot, h, i, 1] + grad * grad
        state[slot, h, i, 1] = summed
        state[slot, h, i, 0] = state[slot, h, i, 0] - LEARN_RATE * grad * lax.rsqrt(summed)

    def update_users():
        def update(u, carry):
            span = pl.ds(pl.multiple_of(u * block, block), block)
            now = users[span]
            grad = grad_users[span] + DECAY * now
            summed = user_accum[span] + grad * grad
            user_accum[span] = summed
            now = now - LEARN_RATE * grad * lax.rsqrt(summed)
            users[span] = now
            ub[span] = now.astype(BF16)
            return carry

        lax.fori_loop(0, n_users // block, update, 0, unroll=True)

    def pass_on(s, h, i):
        first_hop(s, h, i).wait_recv()
        second_hop(s, h, i).start()

    stores = []
    for s in range(SUBS):
        masks(s)
        if s == 0:
            loads[0].wait()
            ub[...] = users[...].astype(BF16)
        else:

            @pl.when(parity == 0)
            def _(s=s):
                for h in range(2):
                    pass_on(s - 1, h, 1)

        for h in range(2):
            if s > 0:

                @pl.when(parity == 1)
                def _(s=s, h=h):
                    pass_on(s - 1, h, 0)

                for i in range(PARTS):
                    direct(s - 1, h, i).wait_recv()
            else:
                for load in loads[8 + 4 * h : 12 + 4 * h]:
                    load.wait()
            work(h, s)
            for i in range(PARTS):
                adagrad(s, h, i)
                if s == 0 and h == 0 and i == 0:
                    pl.semaphore_wait(barrier, 6 - 2 * parity)
                if s < SUBS - 1:

                    @pl.when(parity == 0)
                    def _(s=s, h=h, i=i):
                        direct(s, h, i).start()

                    @pl.when(parity == 1)
                    def _(s=s, h=h, i=i):
                        first_hop(s, h, i).start()

                else:
                    to_rows = pl.ds(h * half + i * size, size)
                    for k, target in enumerate((items_out, item_accum_out)):
                        store = pltpu.make_async_copy(
                            state.at[s, h, i, k],
                            target.at[to_rows],
                            store_sem.at[2 + 4 * h + 2 * i + k],
                        )
                        store.start()
                        stores.append(store)
        if s == 0:
            loads[1].wait()
        update_users()
    for i, (source, target) in enumerate(
        ((users, users_out), (user_accum, user_accum_out))
    ):
        store = pltpu.make_async_copy(source, target, store_sem.at[i])
        store.start()
        stores.append(store)

    for s in range(SUBS - 1):
        for h in range(2):
            for i in range(PARTS):
                direct(s, h, i).wait_send()
            second_hop(s, h, 0).wait_send()
    for store in stores:
        store.wait()


def write_out(*refs):
    sources, targets, buffers, (load_sem, store_sem) = (
        refs[:4],
        refs[4:8],
        refs[8:12],
        refs[12:],
    )
    loads, stores = [], []
    for i, (source, target, buffer) in enumerate(zip(sources, targets, buffers)):
        n = source.shape[0] // PARTS
        for part in range(PARTS):
            span = pl.ds(part * n, n)
            sems = load_sem.at[i, part], store_sem.at[i, part]
            loads.append(
                pltpu.make_async_copy(source.at[span], buffer.at[span], sems[0])
            )
            stores.append(
                pltpu.make_async_copy(buffer.at[span], target.at[span], sems[1])
            )
    for load in loads:
        load.start()
    for load, store in zip(loads, stores):
        load.wait()
        store.start()
    for store in stores:
        store.wait()


def per_device(n_blk, *args):
    users, _, items = args[:3]
    n_users, width = users.shape
    n_items = items.shape[0]
    half = n_items // 2
    entries = -(-(args[4].shape[1] + args[8].shape[1]) // 16) * 16
    anywhere = pl.BlockSpec(memory_space=pl.ANY)
    flops = SUBS * 2 * 3 * n_users * n_items * width
    results = pl.pallas_call(
        functools.partial(kernel, n_blk),
        out_shape=(
            jax.ShapeDtypeStruct(users.shape, F32),
            jax.ShapeDtypeStruct(users.shape, F32),
            jax.ShapeDtypeStruct(items.shape, F32),
            jax.ShapeDtypeStruct(items.shape, F32),
        ),
        in_specs=[anywhere] * 10,
        out_specs=(anywhere,) * 4,
        scratch_shapes=[
            pltpu.VMEM((n_users, width), F32),
            pltpu.VMEM((n_users, width), F32),
            pltpu.VMEM((SUBS, 2, PARTS, 2, half // PARTS, width), F32),
            pltpu.VMEM((SUBS - 1, 2, 2, half // PARTS, width), F32),
            pltpu.VMEM((n_users, width), BF16),
            pltpu.VMEM((half, width), BF16),
            pltpu.VMEM((n_users, width), F32),
            pltpu.VMEM((half, width), F32),
            pltpu.VMEM((entries, n_users), BF16),
            pltpu.VMEM((entries, n_items), BF16),
            pltpu.VMEM((n_users, n_items), BF16),
            pltpu.VMEM((n_users, n_items), BF16),
            *[pltpu.VMEM(arg.shape, arg.dtype) for arg in args[4:]],
            pltpu.SemaphoreType.DMA((SUBS - 1, 2, PARTS)),
            pltpu.SemaphoreType.DMA((SUBS - 1, 2, PARTS)),
            pltpu.SemaphoreType.DMA((SUBS - 1, 2)),
            pltpu.SemaphoreType.DMA((SUBS - 1, 2)),
            pltpu.SemaphoreType.DMA((8 + 4 * PARTS,)),
            pltpu.SemaphoreType.DMA((2 + 4 * PARTS,)),
        ],
        compiler_params=pltpu.CompilerParams(
            collective_id=0, has_side_effects=True, vmem_limit_bytes=56 * 2**20
        ),
        cost_estimate=pl.CostEstimate(
            flops=flops, bytes_accessed=12 * 2**20, transcendentals=0
        ),
    )(*args)
    return pl.pallas_call(
        write_out,
        out_shape=[jax.ShapeDtypeStruct(x.shape, x.dtype) for x in results],
        in_specs=[anywhere] * 4,
        out_specs=[anywhere] * 4,
        scratch_shapes=[
            *[pltpu.VMEM(x.shape, x.dtype) for x in results],
            pltpu.SemaphoreType.DMA((4, PARTS)),
            pltpu.SemaphoreType.DMA((4, PARTS)),
        ],
        compiler_params=pltpu.CompilerParams(vmem_limit_bytes=56 * 2**20),
        cost_estimate=pl.CostEstimate(
            flops=0, bytes_accessed=6 * 2**20, transcendentals=0
        ),
    )(*results)


def solution(mesh):
    flat = P(("blk", "xor"), None)
    tiles = P(None, ("blk", "xor"))
    live = P(None, ("blk", "xor"), None)
    return jax.shard_map(
        functools.partial(per_device, mesh.shape["blk"]),
        mesh=mesh,
        in_specs=(flat, flat, flat, flat, tiles, tiles, live, live, tiles, tiles),
        out_specs=(flat, flat, flat, flat),
        check_vma=False,
    )
```

```python
import functools

import jax
import jax.numpy as jnp
from jax import lax
from jax.experimental import pallas as pl
from jax.experimental.pallas import tpu as pltpu
from jax.sharding import PartitionSpec as P

SUBS = 6
TILE = 128
LEARN_RATE = 0.05
DECAY = 0.02
NEG_WEIGHT = 0.25
PARTS = 2
MESH = pl.DeviceIdType.MESH
F32 = jnp.float32
BF16 = jnp.bfloat16


def flipped(index, bit):
    step = 2**bit
    return index + step - 2 * step * ((index // step) % 2)


def as_column(row):
    n = row.shape[1]
    full = jnp.broadcast_to(row, (n, n))
    diagonal = lax.broadcasted_iota(jnp.int32, (n, n), 0) == lax.broadcasted_iota(
        jnp.int32, (n, n), 1
    )
    return jnp.sum(jnp.where(diagonal, full, 0), axis=1, keepdims=True)


def one_hot_rows(column, live, tiles):
    return jnp.concatenate(
        [jnp.where(column == tile, live, 0.0) for tile in range(tiles)], axis=1
    )


def dot(a, b, ca, cb):
    return lax.dot_general(a, b, (((ca,), (cb,)), ((), ())), preferred_element_type=F32)


def kernel(
    n_blk,
    users_in,
    user_accum_in,
    items_in,
    item_accum_in,
    seen_user_in,
    seen_item_in,
    row_live_in,
    col_live_in,
    neg_user_in,
    neg_item_in,
    users_out,
    user_accum_out,
    items_out,
    item_accum_out,
    users,
    user_accum,
    state,
    lent,
    made,
    given,
    relay,
    ub,
    vb,
    grad_users,
    grad_items,
    rows,
    cols,
    weight,
    seen,
    seen_user_ref,
    seen_item_ref,
    row_live_ref,
    col_live_ref,
    neg_user_ref,
    neg_item_ref,
    send_sem,
    recv_sem,
    relay_send,
    relay_recv,
    load_sem,
    store_sem,
):
    blk = lax.axis_index("blk")
    xor = lax.axis_index("xor")
    parity = lax.rem(blk, 2)

    def at(by):
        return lax.rem(blk + n_blk + by, n_blk)

    swap0, swap1 = flipped(xor, 0), flipped(xor, 1)
    swap01 = flipped(swap0, 1)
    barrier = pltpu.get_barrier_semaphore()

    def greet(by, others):
        for other in others:
            pl.semaphore_signal(
                barrier, inc=1, device_id=(at(by), other), device_id_type=MESH
            )

    greet(-2, (xor, swap1, swap01))
    greet(-1, (xor, swap0, swap1))

    @pl.when(parity == 0)
    def _():
        greet(1, (xor, swap1))

    n_users, width = users_in.shape
    half = items_in.shape[0] // 2
    block = 256
    n_obs = seen_user_ref.shape[1]
    n_neg = neg_user_ref.shape[1]
    pad = rows.shape[0] - n_obs - n_neg

    halves = [pl.ds(h * half, half) for h in range(2)]
    pairs = (
        (users_in, users),
        (items_in.at[halves[0]], state.at[0, 0, 0]),
        (seen_user_in, seen_user_ref),
        (seen_item_in, seen_item_ref),
        (row_live_in, row_live_ref),
        (col_live_in, col_live_ref),
        (neg_user_in, neg_user_ref),
        (neg_item_in, neg_item_ref),
        (item_accum_in.at[halves[0]], state.at[0, 0, 1]),
        (items_in.at[halves[1]], state.at[0, 1, 0]),
        (item_accum_in.at[halves[1]], state.at[0, 1, 1]),
        (user_accum_in, user_accum),
    )
    loads = [
        pltpu.make_async_copy(source, target, load_sem.at[i])
        for i, (source, target) in enumerate(pairs)
    ]
    for load in loads:
        load.start()
    for load in loads[2:8]:
        load.wait()

    def masks(s):
        user_tiles, item_tiles = n_users // TILE, 2 * half // TILE
        root = jnp.full((n_neg, TILE), NEG_WEIGHT**0.5, F32)
        for index, negative, live, out, tiles in (
            (seen_user_ref, neg_user_ref, row_live_ref, rows, user_tiles),
            (seen_item_ref, neg_item_ref, col_live_ref, cols, item_tiles),
        ):
            observed = one_hot_rows(
                as_column(index[pl.ds(s, 1), :]), live[s].astype(F32), tiles
            )
            sampled = one_hot_rows(as_column(negative[pl.ds(s, 1), :]), root, tiles)
            out[...] = jnp.concatenate(
                [observed, sampled, jnp.zeros((pad, tiles * TILE), F32)], axis=0
            ).astype(BF16)

        def spread(u, carry):
            span = pl.ds(pl.multiple_of(u * block, block), block)
            weight[span] = dot(rows[:, span], cols[...], 0, 0).astype(BF16)
            seen[span] = dot(rows[:n_obs, span], cols[:n_obs], 0, 0).astype(BF16)
            return carry

        lax.fori_loop(0, n_users // block, spread, 0)

    def remote(source, target, kind, c, h, device, part=0):
        return pltpu.make_async_remote_copy(
            src_ref=source,
            dst_ref=target,
            send_sem=send_sem.at[c, kind, h, part],
            recv_sem=recv_sem.at[c, kind, h, part],
            device_id=device,
            device_id_type=MESH,
        )

    spans = [pl.ds(i * (half // PARTS), half // PARTS) for i in range(PARTS)]

    def factor_on(c, h, i):
        to = (at(2), xor if h == 0 else swap01)
        source, target = state.at[c, h, 0, spans[i]], state.at[c + 1, h, 0, spans[i]]
        return remote(source, target, 0, c, h, to, i)

    def accum_on(c, h):
        to = (at(2), xor if h == 0 else swap01)
        return remote(state.at[c, h, 1], state.at[c + 1, h, 1], 1, c, h, to)

    def lend(c, h, i):
        to = (at(1), xor if h == 0 else swap0)
        source, target = state.at[c, h, 0, spans[i]], lent.at[c, h, spans[i]]
        return remote(source, target, 2, c, h, to, i)

    def lend_back(c, h, i):
        to = (at(-1), xor if h == 0 else swap1)
        source, target = state.at[c + 1, h, 0, spans[i]], lent.at[c, h, spans[i]]
        return remote(source, target, 2, c, h, to, i)

    def give_grad(c, h):
        to = (at(1), xor if h == 0 else swap1)
        return remote(made.at[c, h], given.at[c, h], 3, c, h, to)

    def grad_hop(c, h):
        to = (at(2) if h == 0 else at(-1), xor)
        return pltpu.make_async_remote_copy(
            src_ref=made.at[c, h],
            dst_ref=relay.at[c],
            send_sem=send_sem.at[c, 3, h, 0],
            recv_sem=relay_recv.at[c],
            device_id=to,
            device_id_type=MESH,
        )

    def remote_pass(c):
        return pltpu.make_async_remote_copy(
            src_ref=relay.at[c],
            dst_ref=given.at[c, 0],
            send_sem=relay_send.at[c],
            recv_sem=recv_sem.at[c, 3, 0, 0],
            device_id=(at(-1), xor),
            device_id_type=MESH,
        )

    def pass_grad(c, h):
        grad_hop(c, h).wait_recv()
        to = (at(-1), xor) if h == 0 else (at(2), swap1)
        pltpu.make_async_remote_copy(
            src_ref=relay.at[c],
            dst_ref=given.at[c, h],
            send_sem=relay_send.at[c],
            recv_sem=recv_sem.at[c, 3, h, 0],
            device_id=to,
            device_id_type=MESH,
        ).start()

    def last_move(h, kind):
        to = (at(1), xor if h == 0 else swap0)
        return remote(state.at[2, h, kind], state.at[3, h, kind], kind, 2, h, to)

    def work(h, factor, grad):
        vb[...] = factor[...].astype(BF16)
        grad[...] = DECAY * factor[...]

        def terms(u, carry):
            span = pl.ds(pl.multiple_of(u * block, block), block)
            scores = dot(ub[span], vb[...], 1, 1)
            weighted = weight[span, halves[h]].astype(F32) * scores
            err = (weighted - seen[span, halves[h]].astype(F32)).astype(BF16)
            user_terms = dot(err, vb[...], 1, 0)
            if h == 0:
                grad_users[span] = user_terms
            else:
                grad_users[span] += user_terms
            grad[...] += dot(err, ub[span], 0, 0)
            return carry

        lax.fori_loop(0, n_users // block, terms, 0, unroll=True)

    def adagrad(factor, accum, grad_ref):
        grad = grad_ref[...]
        summed = accum[...] + grad * grad
        accum[...] = summed
        factor[...] = factor[...] - LEARN_RATE * grad * lax.rsqrt(summed)

    def update_users():
        def update(u, carry):
            span = pl.ds(pl.multiple_of(u * block, block), block)
            now = users[span]
            grad = grad_users[span] + DECAY * now
            summed = user_accum[span] + grad * grad
            user_accum[span] = summed
            now = now - LEARN_RATE * grad * lax.rsqrt(summed)
            users[span] = now
            ub[span] = now.astype(BF16)
            return carry

        lax.fori_loop(0, n_users // block, update, 0, unroll=True)

    cycles = SUBS // 2 - 1
    for c in range(cycles + 1):
        masks(2 * c)
        if c == 0:
            loads[0].wait()
            ub[...] = users[...].astype(BF16)
        for h in range(2):
            factor, accum = state.at[c, h, 0], state.at[c, h, 1]
            if c == 0:
                loads[1 if h == 0 else 9].wait()
            else:
                accum_on(c - 1, h).wait_recv()
                for i in range(PARTS):
                    lend(c - 1, h, i).wait_send()
                give_grad(c - 1, h).wait_recv()
                adagrad(factor, accum, given.at[c - 1, h])
            work(h, factor, grad_items.at[h])
            if c == 0:
                loads[8 if h == 0 else 10].wait()
            adagrad(factor, accum, grad_items.at[h])
            if c == 0 and h == 0:
                pl.semaphore_wait(barrier, 6 + 2 * parity)
            if c == cycles:
                last_move(h, 0).start()
            else:

                @pl.when(parity == 0)
                def _(c=c, h=h):
                    for i in range(PARTS):
                        lend(c, h, i).start()

                for i in range(PARTS):
                    factor_on(c, h, i).start()
        if c == 0:
            loads[11].wait()
        update_users()
        if c == cycles:
            break

        masks(2 * c + 1)
        for h in range(2):
            for i in range(PARTS):
                factor_on(c, h, i).wait_recv()

                @pl.when(parity == 1)
                def _(c=c, h=h, i=i):
                    lend_back(c, h, i).start()

            if h == 1:
                for k in range(2):
                    for i in range(PARTS):
                        factor_on(c, k, i).wait_send()
                for k in range(2):
                    accum_on(c, k).start()
            for i in range(PARTS):
                lend(c, h, i).wait_recv()
            work(h, lent.at[c, h], made.at[c, h])

            @pl.when(parity == 0)
            def _(c=c, h=h):
                give_grad(c, h).start()

            @pl.when(parity == 1)
            def _(c=c, h=h):
                grad_hop(c, h).start()

        update_users()

        @pl.when(parity == 0)
        def _(c=c):
            pass_grad(c, 1)

        @pl.when(parity == 1)
        def _(c=c):
            pass_grad(c, 0)


    masks(SUBS - 1)
    for h in range(2):
        last_move(h, 0).wait_send()
        last_move(h, 1).start()
        last_move(h, 0).wait_recv()
        work(h, state.at[cycles + 1, h, 0], grad_items.at[h])
    update_users()
    stores = [
        pltpu.make_async_copy(users, users_out, store_sem.at[0]),
        pltpu.make_async_copy(user_accum, user_accum_out, store_sem.at[1]),
    ]
    for store in stores:
        store.start()
    for h in range(2):
        last_move(h, 1).wait_recv()
        factor, accum = state.at[cycles + 1, h, 0], state.at[cycles + 1, h, 1]
        adagrad(factor, accum, grad_items.at[h])
        for i, (source, target) in enumerate(
            ((factor, items_out), (accum, item_accum_out))
        ):
            store = pltpu.make_async_copy(
                source, target.at[halves[h]], store_sem.at[2 + 2 * h + i]
            )
            store.start()
            stores.append(store)

    for h in range(2):
        for c in range(cycles):
            accum_on(c, h).wait_send()
            if h == 0:
                remote_pass(c).wait_send()
            give_grad(c, h).wait_send()
        last_move(h, 1).wait_send()
    for store in stores:
        store.wait()


def write_out(*refs):
    sources, targets, buffers, (load_sem, store_sem) = (
        refs[:4],
        refs[4:8],
        refs[8:12],
        refs[12:],
    )
    loads, stores = [], []
    for i, (source, target, buffer) in enumerate(zip(sources, targets, buffers)):
        n = source.shape[0] // PARTS
        for part in range(PARTS):
            span = pl.ds(part * n, n)
            sems = load_sem.at[i, part], store_sem.at[i, part]
            loads.append(
                pltpu.make_async_copy(source.at[span], buffer.at[span], sems[0])
            )
            stores.append(
                pltpu.make_async_copy(buffer.at[span], target.at[span], sems[1])
            )
    for load in loads:
        load.start()
    for load, store in zip(loads, stores):
        load.wait()
        store.start()
    for store in stores:
        store.wait()


def per_device(n_blk, *args):
    users, _, items = args[:3]
    n_users, width = users.shape
    n_items = items.shape[0]
    half = n_items // 2
    entries = -(-(args[4].shape[1] + args[8].shape[1]) // 16) * 16
    anywhere = pl.BlockSpec(memory_space=pl.ANY)
    flops = SUBS * 2 * 3 * n_users * n_items * width
    results = pl.pallas_call(
        functools.partial(kernel, n_blk),
        out_shape=(
            jax.ShapeDtypeStruct(users.shape, F32),
            jax.ShapeDtypeStruct(users.shape, F32),
            jax.ShapeDtypeStruct(items.shape, F32),
            jax.ShapeDtypeStruct(items.shape, F32),
        ),
        in_specs=[anywhere] * 10,
        out_specs=(anywhere,) * 4,
        scratch_shapes=[
            pltpu.VMEM((n_users, width), F32),
            pltpu.VMEM((n_users, width), F32),
            pltpu.VMEM((SUBS // 2 + 1, 2, 2, half, width), F32),
            *[pltpu.VMEM((SUBS // 2 - 1, 2, half, width), F32)] * 3,
            pltpu.VMEM((SUBS // 2 - 1, half, width), F32),
            pltpu.VMEM((n_users, width), BF16),
            pltpu.VMEM((half, width), BF16),
            pltpu.VMEM((n_users, width), F32),
            pltpu.VMEM((2, half, width), F32),
            pltpu.VMEM((entries, n_users), BF16),
            pltpu.VMEM((entries, n_items), BF16),
            pltpu.VMEM((n_users, n_items), BF16),
            pltpu.VMEM((n_users, n_items), BF16),
            *[pltpu.VMEM(arg.shape, arg.dtype) for arg in args[4:]],
            pltpu.SemaphoreType.DMA((SUBS // 2, 4, 2, PARTS)),
            pltpu.SemaphoreType.DMA((SUBS // 2, 4, 2, PARTS)),
            pltpu.SemaphoreType.DMA((SUBS // 2 - 1,)),
            pltpu.SemaphoreType.DMA((SUBS // 2 - 1,)),
            pltpu.SemaphoreType.DMA((12,)),
            pltpu.SemaphoreType.DMA((6,)),
        ],
        compiler_params=pltpu.CompilerParams(
            collective_id=0, has_side_effects=True, vmem_limit_bytes=56 * 2**20
        ),
        cost_estimate=pl.CostEstimate(
            flops=flops, bytes_accessed=12 * 2**20, transcendentals=0
        ),
    )(*args)
    return pl.pallas_call(
        write_out,
        out_shape=[jax.ShapeDtypeStruct(x.shape, x.dtype) for x in results],
        in_specs=[anywhere] * 4,
        out_specs=[anywhere] * 4,
        scratch_shapes=[
            *[pltpu.VMEM(x.shape, x.dtype) for x in results],
            pltpu.SemaphoreType.DMA((4, PARTS)),
            pltpu.SemaphoreType.DMA((4, PARTS)),
        ],
        compiler_params=pltpu.CompilerParams(vmem_limit_bytes=56 * 2**20),
        cost_estimate=pl.CostEstimate(
            flops=0, bytes_accessed=6 * 2**20, transcendentals=0
        ),
    )(*results)


def solution(mesh):
    flat = P(("blk", "xor"), None)
    tiles = P(None, ("blk", "xor"))
    live = P(None, ("blk", "xor"), None)
    return jax.shard_map(
        functools.partial(per_device, mesh.shape["blk"]),
        mesh=mesh,
        in_specs=(flat, flat, flat, flat, tiles, tiles, live, live, tiles, tiles),
        out_specs=(flat, flat, flat, flat),
        check_vma=False,
    )
```
